32 devices in a mesh: ctx: 16 (over z, x, core), head: 2 (over y).
Axes of the slice: x: 2, y: 2, z: 4, core: 2. Of those that a mesh axis runs over, the one named last changes fastest.
Arguments:
- queries: bfloat16 [4096, 6144], P(('ctx', 'head')), may hold values from -32 to 32
- keys: bfloat16 [4096, 6144], P(('ctx', 'head')), may hold values from -12 to 12
- values: bfloat16 [4096, 6144], P(('ctx', 'head')), may hold values from -6 to 6
- cache_keys: bfloat16 [8192, 6144], P('ctx', 'head'), may hold values from -6 to 6
- cache_values: bfloat16 [8192, 6144], P('ctx', 'head'), may hold values from -6 to 6
- pattern: int32 [32, 4], replicated, may hold values from 0 to 63, as said below
- reached: int32 [32], replicated, may hold values from 1 to 4, as said below
- gate: float32 [6144], replicated, may hold values from 0.5 to 2
Outputs:
- mixed: bfloat16 [4096, 6144], P(('ctx', 'head'))
The draws below stay inside these ranges and needn't reach their ends.
Inputs may be any that keep to these rules, and one draw needn't show every extreme that they name: `pattern`: every entry of row g names a cached tile of ctx index g // 2 - 1, g // 2 or g // 2 + 1, where ctx index c holds cached tiles c * 4 to (c + 1) * 4 - 1. Only the first reached[g] entries of row g of pattern are used.
All inputs are finite; a program needn't handle non-finite values.
Results may differ from the reference program's by a relative error of at most 0.011.
Values may be sent and summed in bfloat16 or wider, within the bound.
A program may use at most 128 MiB of HBM per device.

```python
import jax
import jax.numpy as jnp
from jax import lax

D = 6144
HEADS = 48
HD = 128
TILE = 128
REACH = 4
CT_DEV = 4
QT_DEV = 2
QTILES = 32
CTILES = 64
TOKENS = 4096
N_CTX = 16


def query_key_pair(key):
    base = jax.random.fold_in(key, 7)
    first, second = jax.random.split(base, 2)
    keys_drawn = jnp.clip(jax.random.normal(first, (TOKENS, D), jnp.float32), -6.0, 6.0)
    queries_drawn = jnp.clip(jax.random.normal(second, (TOKENS, D), jnp.float32), -6.0, 6.0)
    return (queries_drawn, keys_drawn)


def draw_queries(key, part):
    return query_key_pair(key)[0].astype(jnp.bfloat16)


def draw_keys(key, part):
    return query_key_pair(key)[1].astype(jnp.bfloat16)


def draw_pattern(key, part):
    tile_ids = jnp.arange(QTILES, dtype=jnp.int32)
    owner = tile_ids // QT_DEV
    lowest = jnp.maximum(owner - 1, 0) * CT_DEV
    highest = jnp.minimum(owner + 2, N_CTX) * CT_DEV
    raw_ids = jax.random.randint(jax.random.fold_in(key, 21), (QTILES, REACH), 0, 1 << 20)
    chosen_ids = lowest[:, None] + raw_ids % (highest - lowest)[:, None]
    chosen_ids = chosen_ids.at[0, 0].set(0)
    chosen_ids = chosen_ids.at[QTILES - 1, 0].set(CTILES - 1)
    return chosen_ids.astype(jnp.int32)


def draw_reached(key, part):
    counts = jax.random.randint(jax.random.fold_in(key, 33), (QTILES,), 1, REACH + 1)
    counts = counts.at[0].set(REACH)
    counts = counts.at[1].set(1)
    return counts.astype(jnp.int32)


def block_scale(rng, dims, shards, low, largest):
    loudness = 1.0
    for axis_at, parts in shards:
        steps = jax.random.uniform(jax.random.fold_in(jax.random.fold_in(rng, 6), axis_at), (parts,), jnp.float32, low / len(shards), largest / len(shards))
        loudness = loudness * jnp.repeat(jnp.exp(steps), dims[axis_at] // parts).reshape((-1,) + (1,) * (len(dims) - 1 - axis_at))
    return loudness


def centred(key, dims, spread, reach, pieces=(), kind=jnp.bfloat16):
    factor_of = block_scale(key, dims, pieces, -0.22, 0.18) if pieces else 1.0
    entries = jax.random.normal(key, dims, jnp.float32) * spread * factor_of
    return jnp.minimum(jnp.maximum(entries, -reach), reach).astype(kind)


def setup_inputs(seed: int = 0) -> dict:
    seeds = jax.random.split(jax.random.key(seed), 9)
    queries = draw_queries(jax.random.fold_in(seeds[8], 71), 0)
    keys = draw_keys(jax.random.fold_in(seeds[8], 71), 0)
    values = centred(seeds[2], (TOKENS, D), 1.0, 6.0, ((0, 32),))
    cache_keys = centred(seeds[3], (CTILES * TILE, D), 1.0, 6.0, ((0, 16), (1, 2)))
    cache_values = centred(seeds[4], (CTILES * TILE, D), 1.0, 6.0, ((0, 16), (1, 2)))
    pattern = draw_pattern(jax.random.fold_in(seeds[8], 71), 0)
    reached = draw_reached(jax.random.fold_in(seeds[8], 71), 0)
    gate = jnp.clip(jax.random.uniform(seeds[7], (D,), jnp.float32, 0.5, 2.0), 0.5, 2.0)
    return {"queries": queries, "keys": keys, "values": values, "cache_keys": cache_keys, "cache_values": cache_values, "pattern": pattern, "reached": reached, "gate": gate}


def reference(queries, keys, values, cache_keys, cache_values, pattern, reached, gate):
    score_scale = HD ** -0.5
    q_all = queries.reshape(QTILES, TILE, HEADS, HD)
    k_all = keys.reshape(QTILES, TILE, HEADS, HD)
    v_all = values.reshape(QTILES, TILE, HEADS, HD)
    cached_k = cache_keys.reshape(CTILES, TILE, HEADS, HD)
    cached_v = cache_values.reshape(CTILES, TILE, HEADS, HD)
    offsets = jnp.arange(-2, 3, dtype=jnp.int32)
    slot_ids = jnp.arange(REACH, dtype=jnp.int32)

    def one_tile(tile_index):
        near_ids = tile_index + offsets
        near_ok = (near_ids >= 0) & (near_ids < QTILES)
        near_ids = jnp.clip(near_ids, 0, QTILES - 1).astype(jnp.int32)
        row_ids = pattern[tile_index].astype(jnp.int32)
        key_blocks = jnp.concatenate([k_all[near_ids], cached_k[row_ids]], axis=0).astype(jnp.float32)
        value_blocks = jnp.concatenate([v_all[near_ids], cached_v[row_ids]], axis=0).astype(jnp.float32)
        usable_keys = jnp.concatenate([near_ok, slot_ids < reached[tile_index]])
        scores = jnp.einsum("qhd,nkhd->hqnk", q_all[tile_index].astype(jnp.float32), key_blocks,
                            precision=lax.Precision.HIGHEST) * score_scale
        keep_mask = usable_keys[None, None, :, None]
        scores = jnp.where(keep_mask, scores, -jnp.inf)
        row_peak = jnp.max(scores, axis=(2, 3), keepdims=True)
        expos = jnp.exp(scores - row_peak)
        row_total = jnp.sum(expos, axis=(2, 3))
        weights = expos.astype(jnp.bfloat16).astype(jnp.float32)
        summed = jnp.einsum("hqnk,nkhd->qhd", weights, value_blocks, precision=lax.Precision.HIGHEST)
        return (summed / jnp.transpose(row_total)[:, :, None]).reshape(TILE, HEADS * HD)

    attended = lax.map(one_tile, jnp.arange(QTILES, dtype=jnp.int32))
    return (attended.reshape(TOKENS, D) * gate).astype(jnp.bfloat16)
```

```python
import functools
import math

import jax
import jax.numpy as jnp
from jax import lax
from jax.experimental import pallas as pl
from jax.experimental.pallas import tpu as pltpu
from jax.sharding import PartitionSpec as P

HD = 128
TILE = 128
REACH = 4
NEGATIVE = -1e30
LOG2E = math.log2(math.e)
GROUP = 2
AHEAD = 3
NT = (((1,), (1,)), ((), ()))
NN = (((1,), (0,)), ((), ()))


def kernel(sizes, q_ref, k_ref, v_ref, ck_ref, cv_ref, pattern_ref, reached_ref, gate_ref, out_ref,
           qs, ks, vs, cks, cvs, qn, po, pi, lo, li, oacc, macc, lacc, ob, bias,
           loc_sem, y_ssem, y_rsem, n_ssem, n_rsem, p_ssem, p_rsem, l_ssem, l_rsem, o_ssem, o_rsem, oloc_sem):
    n_ctx, n_head, rows, width, cw, hc, nch, tiles_here, cache_tiles = sizes
    c = lax.axis_index("ctx")
    h = lax.axis_index("head")
    has = (c > 0, c < n_ctx - 1)
    side_id = (c - 1, c + 1)
    all_rows = n_head * rows

    def at_head(d):
        return lax.rem(h + d, n_head)

    def from_head(d):
        return lax.rem(h - d + n_head, n_head)

    def row_block(i):
        return pl.ds(pl.multiple_of(i * rows, rows), rows)

    def columns(i, j):
        return pl.ds(pl.multiple_of(i * width + j * cw, cw), cw)

    def local_in(j):
        mine = row_block(h)
        pairs = [
            (q_ref.at[:, columns(h, j)], qs.at[j, mine, :]),
            (k_ref.at[:, columns(h, j)], ks.at[j, mine, :]),
            (v_ref.at[:, columns(h, j)], vs.at[j, mine, :]),
            (ck_ref.at[:, columns(0, j)], cks.at[j]),
            (cv_ref.at[:, columns(0, j)], cvs.at[j]),
        ]
        return [pltpu.make_async_copy(s, t, loc_sem.at[n, j]) for n, (s, t) in enumerate(pairs)]

    def exchange(t, d, j):
        src = (q_ref, k_ref, v_ref)[t]
        dst = (qs, ks, vs)[t]
        to = at_head(d)
        return pltpu.make_async_remote_copy(
            src_ref=src.at[:, columns(to, j)], dst_ref=dst.at[j, row_block(h), :],
            send_sem=y_ssem.at[t, d - 1, j], recv_sem=y_rsem.at[t, d - 1, j],
            device_id=(c, to), device_id_type=pl.DeviceIdType.MESH)

    def exchange_in(t, d, j):
        dst = (qs, ks, vs)[t].at[j, row_block(from_head(d)), :]
        return pltpu.make_async_remote_copy(
            src_ref=dst, dst_ref=dst,
            send_sem=y_ssem.at[t, d - 1, j], recv_sem=y_rsem.at[t, d - 1, j],
            device_id=(c, from_head(d)), device_id_type=pl.DeviceIdType.MESH)

    def query_out(s, d, j):
        piece = row_block(from_head(d))
        src = q_ref.at[:, columns(h, j)] if d == 0 else qs.at[j, piece, :]
        return pltpu.make_async_remote_copy(
            src_ref=src, dst_ref=qn.at[1 - s, j, piece, :],
            send_sem=n_ssem.at[s, d, j], recv_sem=n_rsem.at[1 - s, d, j],
            device_id=(side_id[s], h), device_id_type=pl.DeviceIdType.MESH)

    def query_in(s, d, j):
        dst = qn.at[s, j, row_block(from_head(d)), :]
        return pltpu.make_async_remote_copy(
            src_ref=dst, dst_ref=dst,
            send_sem=n_ssem.at[s, d, j], recv_sem=n_rsem.at[s, d, j],
            device_id=(side_id[s], h), device_id_type=pl.DeviceIdType.MESH)

    def part_out(s, j):
        return [
            pltpu.make_async_remote_copy(
                src_ref=src.at[s, j], dst_ref=dst.at[1 - s, j],
                send_sem=ss.at[s, j], recv_sem=rs.at[1 - s, j],
                device_id=(side_id[s], h), device_id_type=pl.DeviceIdType.MESH)
            for src, dst, ss, rs in ((po, pi, p_ssem, p_rsem), (lo, li, l_ssem, l_rsem))
        ]

    def part_in(s, j):
        return [
            pltpu.make_async_remote_copy(
                src_ref=dst.at[s, j], dst_ref=dst.at[s, j],
                send_sem=ss.at[s, j], recv_sem=rs.at[s, j],
                device_id=(side_id[s], h), device_id_type=pl.DeviceIdType.MESH)
            for dst, ss, rs in ((pi, p_ssem, p_rsem), (li, l_ssem, l_rsem))
        ]

    def result_out(d, j):
        to = at_head(d)
        return pltpu.make_async_remote_copy(
            src_ref=ob.at[j, row_block(to), :], dst_ref=out_ref.at[:, columns(h, j)],
            send_sem=o_ssem.at[d - 1, j], recv_sem=o_rsem.at[d - 1, j],
            device_id=(c, to), device_id_type=pl.DeviceIdType.MESH)

    def result_in(d, j):
        dst = out_ref.at[:, columns(from_head(d), j)]
        return pltpu.make_async_remote_copy(
            src_ref=dst, dst_ref=dst,
            send_sem=o_ssem.at[d - 1, j], recv_sem=o_rsem.at[d - 1, j],
            device_id=(c, from_head(d)), device_id_type=pl.DeviceIdType.MESH)

    def result_local(j):
        return pltpu.make_async_copy(
            ob.at[j, row_block(h), :], out_ref.at[:, columns(h, j)], oloc_sem.at[j])

    barrier = pltpu.get_barrier_semaphore()
    for d in range(1, n_head):
        pl.semaphore_signal(barrier, inc=1, device_id=(c, at_head(d)), device_id_type=pl.DeviceIdType.MESH)
    for s in range(2):
        @pl.when(has[s])
        def _():
            pl.semaphore_signal(barrier, inc=1, device_id=(side_id[s], h), device_id_type=pl.DeviceIdType.MESH)

    @pl.loop(0, nch)
    def _(j):
        for copy in local_in(j):
            copy.start()

    for s in range(3):
        source = jnp.clip(c + (-1, 1, 0)[s], 0, n_ctx - 1)
        for t in range(tiles_here):
            g = source * tiles_here + t
            used = reached_ref[g]
            for b in range(tiles_here):
                away = g - (c * tiles_here + b)
                near = jnp.where((away >= -2) & (away <= 2), 0.0, NEGATIVE)
                bias[s, pl.ds(b, 1), pl.ds(t * TILE, TILE)] = jnp.full((1, TILE), near, jnp.float32)
            for b in range(cache_tiles):
                times = jnp.int32(0)
                for r in range(REACH):
                    hit = (pattern_ref[g, r] == c * cache_tiles + b) & (r < used)
                    times = times + jnp.where(hit, 1, 0)
                log = jnp.float32(NEGATIVE)
                for n in range(1, REACH + 1):
                    log = jnp.where(times == n, jnp.float32(math.log2(n)), log)
                bias[s, pl.ds(tiles_here + b, 1), pl.ds(t * TILE, TILE)] = jnp.full((1, TILE), log, jnp.float32)

    peers = n_head - 1 + jnp.where(has[0], 1, 0) + jnp.where(has[1], 1, 0)
    pl.semaphore_wait(barrier, peers)

    def send_chunk(j):
        for t in range(3):
            for d in range(1, n_head):
                exchange(t, d, j).start()
        for s in range(2):
            @pl.when(has[s])
            def _():
                query_out(s, 0, j).start()

    ahead = min(AHEAD, nch)

    @pl.loop(0, ahead)
    def _(j):
        send_chunk(j)

    scale = HD ** -0.5 * LOG2E

    def partial(s, q, k_block, k_cache, v_turned):
        near = lax.dot_general(k_block, q, NT, preferred_element_type=jnp.float32)
        far = lax.dot_general(k_cache, q, NT, preferred_element_type=jnp.float32)
        parts = []
        for b in range(tiles_here + cache_tiles):
            block = near[b * TILE:(b + 1) * TILE] if b < tiles_here else (
                far[(b - tiles_here) * TILE:(b - tiles_here + 1) * TILE])
            parts.append(block * scale + bias[s, pl.ds(b, 1), :])
        scores = jnp.concatenate(parts, axis=0)
        peak = jnp.max(scores, axis=0, keepdims=True)
        expos = jnp.exp2(scores - peak)
        total = jnp.sum(expos, axis=0, keepdims=True)
        summed = lax.dot_general(v_turned, expos.astype(jnp.bfloat16), NN, preferred_element_type=jnp.float32)
        return summed, peak, total

    def relay(j):
        for d in range(1, n_head):
            exchange_in(0, d, j).wait_recv()
            for s in range(2):
                @pl.when(has[s])
                def _():
                    query_out(s, d, j).start()

    def attend(j):
        for copy in local_in(j):
            copy.wait()
        for t in (1, 2):
            for d in range(1, n_head):
                exchange_in(t, d, j).wait_recv()
        for s in range(2):
            @pl.when(has[s])
            def _():
                for d in range(n_head):
                    query_in(s, d, j).wait_recv()
        for i in range(hc):
            cols = slice(i * HD, (i + 1) * HD)
            k_block, k_cache = ks[j, :, cols], cks[j, :, cols]
            v_turned = jnp.concatenate([vs[j, :, cols].T, cvs[j, :, cols].T], axis=1)
            for s in range(2):
                @pl.when(has[s])
                def _():
                    summed, peak, total = partial(s, qn[s, j, :, cols], k_block, k_cache, v_turned)
                    po[s, j, i] = (summed * (1.0 / total)).astype(jnp.bfloat16)
                    lo[s, j, pl.ds(i, 1), :] = peak + jnp.log2(total)
            summed, peak, total = partial(2, qs[j, :, cols], k_block, k_cache, v_turned)
            oacc[j, i] = summed
            macc[j, pl.ds(i, 1), :] = peak
            lacc[j, pl.ds(i, 1), :] = total
        for s in range(2):
            @pl.when(has[s])
            def _():
                for copy in part_out(s, j):
                    copy.start()

    def combine(j):
        for s in range(2):
            @pl.when(has[s])
            def _():
                for copy in part_in(s, j):
                    copy.wait_recv()

            @pl.when(jnp.logical_not(has[s]))
            def _():
                pi[s, j] = jnp.zeros(pi.shape[2:], pi.dtype)
                li[s, j] = jnp.full(li.shape[2:], NEGATIVE, li.dtype)
        for i in range(hc):
            m_own, m_low, m_high = macc[j, pl.ds(i, 1), :], li[0, j, pl.ds(i, 1), :], li[1, j, pl.ds(i, 1), :]
            top = jnp.maximum(m_own, jnp.maximum(m_low, m_high))
            f_own, f_low, f_high = jnp.exp2(m_own - top), jnp.exp2(m_low - top), jnp.exp2(m_high - top)
            inverse = 1.0 / (f_own * lacc[j, pl.ds(i, 1), :] + f_low + f_high)
            mixed = (oacc[j, i] * (f_own * inverse) + pi[0, j, i].astype(jnp.float32) * (f_low * inverse)
                     + pi[1, j, i].astype(jnp.float32) * (f_high * inverse))
            gain = gate_ref[pl.ds(h * (width // HD) + j * hc + i, 1), :]
            ob[j, :, i * HD:(i + 1) * HD] = (mixed.T * gain).astype(jnp.bfloat16)
        for d in range(1, n_head):
            result_out(d, j).start()
        result_local(j).start()

    @pl.loop(0, nch + 2)
    def _(i):
        @pl.when(i + ahead < nch)
        def _():
            send_chunk(i + ahead)

        @pl.when(i < nch)
        def _():
            relay(i)

        @pl.when((i >= 1) & (i <= nch))
        def _():
            attend(i - 1)

        @pl.when(i >= 2)
        def _():
            combine(i - 2)

    @pl.loop(0, nch)
    def _(j):
        for t in range(3):
            for d in range(1, n_head):
                exchange(t, d, j).wait_send()
        for s in range(2):
            @pl.when(has[s])
            def _():
                for d in range(n_head):
                    query_out(s, d, j).wait_send()
                for copy in part_out(s, j):
                    copy.wait_send()
        for d in range(1, n_head):
            result_out(d, j).wait_send()
            result_in(d, j).wait_recv()
        result_local(j).wait()


def local(n_ctx, n_head, queries, keys, values, cache_keys, cache_values, pattern, reached, gate):
    rows, model = queries.shape
    width = cache_keys.shape[1]
    heads_here = width // HD
    hc = max(n for n in range(1, GROUP + 1) if heads_here % n == 0)
    cw = hc * HD
    nch = heads_here // hc
    all_rows = rows * n_head
    tiles_here = all_rows // TILE
    cache_rows = cache_keys.shape[0]
    cache_tiles = cache_rows // TILE
    sizes = (n_ctx, n_head, rows, width, cw, hc, nch, tiles_here, cache_tiles)
    bf, f32 = jnp.bfloat16, jnp.float32
    dma = pltpu.SemaphoreType.DMA
    hbm = pl.BlockSpec(memory_space=pl.ANY)
    smem = pl.BlockSpec(memory_space=pltpu.SMEM)
    own = max(n_head - 1, 1)
    return pl.pallas_call(
        functools.partial(kernel, sizes),
        out_shape=jax.ShapeDtypeStruct((rows, model), bf),
        in_specs=[hbm] * 5 + [smem, smem, pl.BlockSpec(memory_space=pltpu.VMEM)],
        out_specs=hbm,
        scratch_shapes=[
            pltpu.VMEM((nch, all_rows, cw), bf),
            pltpu.VMEM((nch, all_rows, cw), bf),
            pltpu.VMEM((nch, all_rows, cw), bf),
            pltpu.VMEM((nch, cache_rows, cw), bf),
            pltpu.VMEM((nch, cache_rows, cw), bf),
            pltpu.VMEM((2, nch, all_rows, cw), bf),
            pltpu.VMEM((2, nch, hc, HD, all_rows), bf),
            pltpu.VMEM((2, nch, hc, HD, all_rows), bf),
            pltpu.VMEM((2, nch, 8, all_rows), f32),
            pltpu.VMEM((2, nch, 8, all_rows), f32),
            pltpu.VMEM((nch, hc, HD, all_rows), f32),
            pltpu.VMEM((nch, 8, all_rows), f32),
            pltpu.VMEM((nch, 8, all_rows), f32),
            pltpu.VMEM((nch, all_rows, cw), bf),
            pltpu.VMEM((3, -(-(tiles_here + cache_tiles) // 8) * 8, all_rows), f32),
            dma((5, nch)),
            dma((3, own, nch)), dma((3, own, nch)),
            dma((2, n_head, nch)), dma((2, n_head, nch)),
            dma((2, nch)), dma((2, nch)),
            dma((2, nch)), dma((2, nch)),
            dma((own, nch)), dma((own, nch)),
            dma((nch,)),
        ],
        compiler_params=pltpu.CompilerParams(
            collective_id=0, has_side_effects=True, vmem_limit_bytes=56 * 1024 * 1024),
    )(queries, keys, values, cache_keys, cache_values, pattern, reached, gate.reshape(model // HD, HD))


def solution(mesh):
    placed = (
        P(("ctx", "head"), None),
        P(("ctx", "head"), None),
        P(("ctx", "head"), None),
        P("ctx", "head"),
        P("ctx", "head"),
        P(),
        P(),
        P(),
    )
    return jax.shard_map(
        functools.partial(local, mesh.shape["ctx"], mesh.shape["head"]),
        mesh=mesh, in_specs=placed, out_specs=P(("ctx", "head"), None), check_vma=False
    )
```

```python
import functools
import math

import jax
import jax.numpy as jnp
from jax import lax
from jax.experimental import pallas as pl
from jax.experimental.pallas import tpu as pltpu
from jax.sharding import PartitionSpec as P

HD = 128
TILE = 128
REACH = 4
NEGATIVE = -1e30
LOG2E = math.log2(math.e)
GROUP = 4
AHEAD = 3
NT = (((1,), (1,)), ((), ()))
NN = (((1,), (0,)), ((), ()))


def kernel(sizes, q_ref, k_ref, v_ref, ck_ref, cv_ref, pattern_ref, reached_ref, gate_ref, out_ref,
           qs, ks, vs, cks, cvs, qn, po, pi, lo, li, oacc, macc, lacc, ob, bias,
           loc_sem, y_ssem, y_rsem, n_ssem, n_rsem, p_ssem, p_rsem, l_ssem, l_rsem, o_ssem, o_rsem, oloc_sem):
    n_ctx, n_head, rows, width, cw, hc, nch, tiles_here, cache_tiles = sizes
    c = lax.axis_index("ctx")
    h = lax.axis_index("head")
    has = (c > 0, c < n_ctx - 1)
    side_id = (c - 1, c + 1)
    all_rows = n_head * rows

    def at_head(d):
        return lax.rem(h + d, n_head)

    def from_head(d):
        return lax.rem(h - d + n_head, n_head)

    def row_block(i):
        return pl.ds(pl.multiple_of(i * rows, rows), rows)

    def columns(i, j):
        return pl.ds(pl.multiple_of(i * width + j * cw, cw), cw)

    def local_in(j):
        mine = row_block(h)
        pairs = [
            (q_ref.at[:, columns(h, j)], qs.at[j, mine, :]),
            (k_ref.at[:, columns(h, j)], ks.at[j, mine, :]),
            (v_ref.at[:, columns(h, j)], vs.at[j, mine, :]),
            (ck_ref.at[:, columns(0, j)], cks.at[j]),
            (cv_ref.at[:, columns(0, j)], cvs.at[j]),
        ]
        return [pltpu.make_async_copy(s, t, loc_sem.at[n, j]) for n, (s, t) in enumerate(pairs)]

    def exchange(t, d, j):
        src = (q_ref, k_ref, v_ref)[t]
        dst = (qs, ks, vs)[t]
        to = at_head(d)
        return pltpu.make_async_remote_copy(
            src_ref=src.at[:, columns(to, j)], dst_ref=dst.at[j, row_block(h), :],
            send_sem=y_ssem.at[t, d - 1, j], recv_sem=y_rsem.at[t, d - 1, j],
            device_id=(c, to), device_id_type=pl.DeviceIdType.MESH)

    def exchange_in(t, d, j):
        dst = (qs, ks, vs)[t].at[j, row_block(from_head(d)), :]
        return pltpu.make_async_remote_copy(
            src_ref=dst, dst_ref=dst,
            send_sem=y_ssem.at[t, d - 1, j], recv_sem=y_rsem.at[t, d - 1, j],
            device_id=(c, from_head(d)), device_id_type=pl.DeviceIdType.MESH)

    def query_out(s, d, j):
        piece = row_block(from_head(d))
        src = q_ref.at[:, columns(h, j)] if d == 0 else qs.at[j, piece, :]
        return pltpu.make_async_remote_copy(
            src_ref=src, dst_ref=qn.at[1 - s, j, piece, :],
            send_sem=n_ssem.at[s, d, j], recv_sem=n_rsem.at[1 - s, d, j],
            device_id=(side_id[s], h), device_id_type=pl.DeviceIdType.MESH)

    def query_in(s, d, j):
        dst = qn.at[s, j, row_block(from_head(d)), :]
        return pltpu.make_async_remote_copy(
            src_ref=dst, dst_ref=dst,
            send_sem=n_ssem.at[s, d, j], recv_sem=n_rsem.at[s, d, j],
            device_id=(side_id[s], h), device_id_type=pl.DeviceIdType.MESH)

    def part_out(s, j):
        return [
            pltpu.make_async_remote_copy(
                src_ref=src.at[s, j], dst_ref=dst.at[1 - s, j],
                send_sem=ss.at[s, j], recv_sem=rs.at[1 - s, j],
                device_id=(side_id[s], h), device_id_type=pl.DeviceIdType.MESH)
            for src, dst, ss, rs in ((po, pi, p_ssem, p_rsem), (lo, li, l_ssem, l_rsem))
        ]

    def part_in(s, j):
        return [
            pltpu.make_async_remote_copy(
                src_ref=dst.at[s, j], dst_ref=dst.at[s, j],
                send_sem=ss.at[s, j], recv_sem=rs.at[s, j],
                device_id=(side_id[s], h), device_id_type=pl.DeviceIdType.MESH)
            for dst, ss, rs in ((pi, p_ssem, p_rsem), (li, l_ssem, l_rsem))
        ]

    def result_out(d, j):
        to = at_head(d)
        return pltpu.make_async_remote_copy(
            src_ref=ob.at[j, row_block(to), :], dst_ref=out_ref.at[:, columns(h, j)],
            send_sem=o_ssem.at[d - 1, j], recv_sem=o_rsem.at[d - 1, j],
            device_id=(c, to), device_id_type=pl.DeviceIdType.MESH)

    def result_in(d, j):
        dst = out_ref.at[:, columns(from_head(d), j)]
        return pltpu.make_async_remote_copy(
            src_ref=dst, dst_ref=dst,
            send_sem=o_ssem.at[d - 1, j], recv_sem=o_rsem.at[d - 1, j],
            device_id=(c, from_head(d)), device_id_type=pl.DeviceIdType.MESH)

    def result_local(j):
        return pltpu.make_async_copy(
            ob.at[j, row_block(h), :], out_ref.at[:, columns(h, j)], oloc_sem.at[j])

    barrier = pltpu.get_barrier_semaphore()
    for d in range(1, n_head):
        pl.semaphore_signal(barrier, inc=1, device_id=(c, at_head(d)), device_id_type=pl.DeviceIdType.MESH)
    for s in range(2):
        @pl.when(has[s])
        def _():
            pl.semaphore_signal(barrier, inc=1, device_id=(side_id[s], h), device_id_type=pl.DeviceIdType.MESH)

    @pl.loop(0, nch)
    def _(j):
        for copy in local_in(j):
            copy.start()

    for s in range(3):
        source = jnp.clip(c + (-1, 1, 0)[s], 0, n_ctx - 1)
        for t in range(tiles_here):
            g = source * tiles_here + t
            used = reached_ref[g]
            for b in range(tiles_here):
                away = g - (c * tiles_here + b)
                near = jnp.where((away >= -2) & (away <= 2), 0.0, NEGATIVE)
                bias[s, pl.ds(b, 1), pl.ds(t * TILE, TILE)] = jnp.full((1, TILE), near, jnp.float32)
            for b in range(cache_tiles):
                times = jnp.int32(0)
                for r in range(REACH):
                    hit = (pattern_ref[g, r] == c * cache_tiles + b) & (r < used)
                    times = times + jnp.where(hit, 1, 0)
                log = jnp.float32(NEGATIVE)
                for n in range(1, REACH + 1):
                    log = jnp.where(times == n, jnp.float32(math.log2(n)), log)
                bias[s, pl.ds(tiles_here + b, 1), pl.ds(t * TILE, TILE)] = jnp.full((1, TILE), log, jnp.float32)

    peers = n_head - 1 + jnp.where(has[0], 1, 0) + jnp.where(has[1], 1, 0)
    pl.semaphore_wait(barrier, peers)

    for s in range(2):
        @pl.when(jnp.logical_not(has[s]))
        def _():
            @pl.loop(0, nch)
            def _(j):
                qn[s, j] = jnp.zeros(qn.shape[2:], qn.dtype)
                pi[s, j] = jnp.zeros(pi.shape[2:], pi.dtype)
                li[s, j] = jnp.full(li.shape[2:], NEGATIVE, li.dtype)

    def send_chunk(j):
        for t in range(3):
            for d in range(1, n_head):
                exchange(t, d, j).start()
        for s in range(2):
            @pl.when(has[s])
            def _():
                query_out(s, 0, j).start()

    ahead = min(AHEAD, nch)

    @pl.loop(0, ahead)
    def _(j):
        send_chunk(j)

    scale = HD ** -0.5 * LOG2E

    def partial(s, near, far):
        blocks, gains, peak = [], [], None
        for b in range(tiles_here + cache_tiles):
            block = near[b * TILE:(b + 1) * TILE] if b < tiles_here else (
                far[(b - tiles_here) * TILE:(b - tiles_here + 1) * TILE])
            gain = bias[s, pl.ds(b, 1), :]
            tall = jnp.max(block, axis=0, keepdims=True) * scale + gain
            peak = tall if peak is None else jnp.maximum(peak, tall)
            blocks.append(block)
            gains.append(gain)
        total, weights = 0.0, []
        for block, gain in zip(blocks, gains):
            expos = jnp.exp2(block * scale + (gain - peak))
            total = total + jnp.sum(expos, axis=0, keepdims=True)
            weights.append(expos.astype(jnp.bfloat16))
        weights = jnp.concatenate(weights, axis=0)
        return weights, peak, total

    def relay(j):
        for d in range(1, n_head):
            exchange_in(0, d, j).wait_recv()
            for s in range(2):
                @pl.when(has[s])
                def _():
                    query_out(s, d, j).start()

    def attend(j):
        for copy in local_in(j):
            copy.wait()
        for t in (1, 2):
            for d in range(1, n_head):
                exchange_in(t, d, j).wait_recv()
        for s in range(2):
            @pl.when(has[s])
            def _():
                for d in range(n_head):
                    query_in(s, d, j).wait_recv()
        units = [(i, s) for i in range(hc) for s in range(3)]
        turned, raw, soft = {}, {}, {}

        def score(i, s):
            cols = slice(i * HD, (i + 1) * HD)
            if s == 0:
                turned[i] = jnp.concatenate([vs[j, :, cols].T, cvs[j, :, cols].T], axis=1)
            q = qs[j, :, cols] if s == 2 else qn[s, j, :, cols]
            raw[i, s] = (lax.dot_general(ks[j, :, cols], q, NT, preferred_element_type=jnp.float32),
                         lax.dot_general(cks[j, :, cols], q, NT, preferred_element_type=jnp.float32))

        def weigh(i, s):
            soft[i, s] = partial(s, *raw.pop((i, s)))

        def gather(i, s):
            weights, peak, total = soft.pop((i, s))
            summed = lax.dot_general(turned[i], weights, NN, preferred_element_type=jnp.float32)
            if s < 2:
                po[s, j, i] = (summed * (1.0 / total)).astype(jnp.bfloat16)
                lo[s, j, pl.ds(i, 1), :] = peak + jnp.log2(total)
            else:
                oacc[j, i] = summed
                macc[j, pl.ds(i, 1), :] = peak
                lacc[j, pl.ds(i, 1), :] = total

        for n in range(len(units) + 2):
            if n < len(units):
                score(*units[n])
            if n >= 2:
                gather(*units[n - 2])
            if 1 <= n <= len(units):
                weigh(*units[n - 1])
        for s in range(2):
            @pl.when(has[s])
            def _():
                for copy in part_out(s, j):
                    copy.start()

    def combine(j):
        for s in range(2):
            @pl.when(has[s])
            def _():
                for copy in part_in(s, j):
                    copy.wait_recv()
        for i in range(hc):
            m_own, m_low, m_high = macc[j, pl.ds(i, 1), :], li[0, j, pl.ds(i, 1), :], li[1, j, pl.ds(i, 1), :]
            top = jnp.maximum(m_own, jnp.maximum(m_low, m_high))
            f_own, f_low, f_high = jnp.exp2(m_own - top), jnp.exp2(m_low - top), jnp.exp2(m_high - top)
            inverse = 1.0 / (f_own * lacc[j, pl.ds(i, 1), :] + f_low + f_high)
            mixed = (oacc[j, i] * (f_own * inverse) + pi[0, j, i].astype(jnp.float32) * (f_low * inverse)
                     + pi[1, j, i].astype(jnp.float32) * (f_high * inverse))
            gain = gate_ref[pl.ds(h * (width // HD) + j * hc + i, 1), :]
            ob[j, :, i * HD:(i + 1) * HD] = (mixed.T * gain).astype(jnp.bfloat16)
        for d in range(1, n_head):
            result_out(d, j).start()
        result_local(j).start()

    @pl.loop(0, nch + 2)
    def _(i):
        @pl.when(i + ahead < nch)
        def _():
            send_chunk(i + ahead)

        @pl.when(i < nch)
        def _():
            relay(i)

        @pl.when((i >= 1) & (i <= nch))
        def _():
            attend(i - 1)

        @pl.when(i >= 2)
        def _():
            combine(i - 2)

    @pl.loop(0, nch)
    def _(j):
        for t in range(3):
            for d in range(1, n_head):
                exchange(t, d, j).wait_send()
        for s in range(2):
            @pl.when(has[s])
            def _():
                for d in range(n_head):
                    query_out(s, d, j).wait_send()
                for copy in part_out(s, j):
                    copy.wait_send()
        for d in range(1, n_head):
            result_out(d, j).wait_send()
            result_in(d, j).wait_recv()
        result_local(j).wait()


def local(n_ctx, n_head, queries, keys, values, cache_keys, cache_values, pattern, reached, gate):
    rows, model = queries.shape
    width = cache_keys.shape[1]
    heads_here = width // HD
    hc = max(n for n in range(1, GROUP + 1) if heads_here % n == 0)
    cw = hc * HD
    nch = heads_here // hc
    all_rows = rows * n_head
    tiles_here = all_rows // TILE
    cache_rows = cache_keys.shape[0]
    cache_tiles = cache_rows // TILE
    sizes = (n_ctx, n_head, rows, width, cw, hc, nch, tiles_here, cache_tiles)
    bf, f32 = jnp.bfloat16, jnp.float32
    dma = pltpu.SemaphoreType.DMA
    hbm = pl.BlockSpec(memory_space=pl.ANY)
    smem = pl.BlockSpec(memory_space=pltpu.SMEM)
    own = max(n_head - 1, 1)
    return pl.pallas_call(
        functools.partial(kernel, sizes),
        out_shape=jax.ShapeDtypeStruct((rows, model), bf),
        in_specs=[hbm] * 5 + [smem, smem, pl.BlockSpec(memory_space=pltpu.VMEM)],
        out_specs=hbm,
        scratch_shapes=[
            pltpu.VMEM((nch, all_rows, cw), bf),
            pltpu.VMEM((nch, all_rows, cw), bf),
            pltpu.VMEM((nch, all_rows, cw), bf),
            pltpu.VMEM((nch, cache_rows, cw), bf),
            pltpu.VMEM((nch, cache_rows, cw), bf),
            pltpu.VMEM((2, nch, all_rows, cw), bf),
            pltpu.VMEM((2, nch, hc, HD, all_rows), bf),
            pltpu.VMEM((2, nch, hc, HD, all_rows), bf),
            pltpu.VMEM((2, nch, 8, all_rows), f32),
            pltpu.VMEM((2, nch, 8, all_rows), f32),
            pltpu.VMEM((nch, hc, HD, all_rows), f32),
            pltpu.VMEM((nch, 8, all_rows), f32),
            pltpu.VMEM((nch, 8, all_rows), f32),
            pltpu.VMEM((nch, all_rows, cw), bf),
            pltpu.VMEM((3, -(-(tiles_here + cache_tiles) // 8) * 8, all_rows), f32),
            dma((5, nch)),
            dma((3, own, nch)), dma((3, own, nch)),
            dma((2, n_head, nch)), dma((2, n_head, nch)),
            dma((2, nch)), dma((2, nch)),
            dma((2, nch)), dma((2, nch)),
            dma((own, nch)), dma((own, nch)),
            dma((nch,)),
        ],
        compiler_params=pltpu.CompilerParams(
            collective_id=0, has_side_effects=True, vmem_limit_bytes=56 * 1024 * 1024),
    )(queries, keys, values, cache_keys, cache_values, pattern, reached, gate.reshape(model // HD, HD))


def solution(mesh):
    placed = (
        P(("ctx", "head"), None),
        P(("ctx", "head"), None),
        P(("ctx", "head"), None),
        P("ctx", "head"),
        P("ctx", "head"),
        P(),
        P(),
        P(),
    )
    return jax.shard_map(
        functools.partial(local, mesh.shape["ctx"], mesh.shape["head"]),
        mesh=mesh, in_specs=placed, out_specs=P(("ctx", "head"), None), check_vma=False
    )
```

```python
import functools
import math

import jax
import jax.numpy as jnp
from jax import lax
from jax.experimental import pallas as pl
from jax.experimental.pallas import tpu as pltpu
from jax.sharding import PartitionSpec as P

HD = 128
TILE = 128
REACH = 4
NEGATIVE = -1e30
LOG2E = math.log2(math.e)
GROUP = 4
AHEAD = 3
LEAD = 1
NT = (((1,), (1,)), ((), ()))
NN = (((1,), (0,)), ((), ()))


def kernel(sizes, q_ref, k_ref, v_ref, ck_ref, cv_ref, pattern_ref, reached_ref, gate_ref, out_ref,
           qs, ks, vs, cks, cvs, qn, po, pi, lo, li, oacc, macc, lacc, ob, bias,
           loc_sem, y_ssem, y_rsem, n_ssem, n_rsem, p_ssem, p_rsem, l_ssem, l_rsem, o_ssem, o_rsem, oloc_sem):
    n_ctx, n_head, rows, width, cw, hc, nch, tiles_here, cache_tiles = sizes
    c = lax.axis_index("ctx")
    h = lax.axis_index("head")
    has = (c > 0, c < n_ctx - 1)
    side_id = (c - 1, c + 1)
    all_rows = n_head * rows

    def at_head(d):
        return lax.rem(h + d, n_head)

    def from_head(d):
        return lax.rem(h - d + n_head, n_head)

    def row_block(i):
        return pl.ds(pl.multiple_of(i * rows, rows), rows)

    def columns(i, j):
        return pl.ds(pl.multiple_of(i * width + j * cw, cw), cw)

    def local_in(j):
        mine = row_block(h)
        pairs = [
            (q_ref.at[:, columns(h, j)], qs.at[j, mine, :]),
            (k_ref.at[:, columns(h, j)], ks.at[j, mine, :]),
            (v_ref.at[:, columns(h, j)], vs.at[j, mine, :]),
            (ck_ref.at[:, columns(0, j)], cks.at[j]),
            (cv_ref.at[:, columns(0, j)], cvs.at[j]),
        ]
        return [pltpu.make_async_copy(s, t, loc_sem.at[n, j]) for n, (s, t) in enumerate(pairs)]

    def exchange(t, d, j):
        src = (q_ref, k_ref, v_ref)[t]
        dst = (qs, ks, vs)[t]
        to = at_head(d)
        return pltpu.make_async_remote_copy(
            src_ref=src.at[:, columns(to, j)], dst_ref=dst.at[j, row_block(h), :],
            send_sem=y_ssem.at[t, d - 1, j], recv_sem=y_rsem.at[t, d - 1, j],
            device_id=(c, to), device_id_type=pl.DeviceIdType.MESH)

    def exchange_in(t, d, j):
        dst = (qs, ks, vs)[t].at[j, row_block(from_head(d)), :]
        return pltpu.make_async_remote_copy(
            src_ref=dst, dst_ref=dst,
            send_sem=y_ssem.at[t, d - 1, j], recv_sem=y_rsem.at[t, d - 1, j],
            device_id=(c, from_head(d)), device_id_type=pl.DeviceIdType.MESH)

    def query_out(s, d, j):
        piece = row_block(from_head(d))
        src = q_ref.at[:, columns(h, j)] if d == 0 else qs.at[j, piece, :]
        return pltpu.make_async_remote_copy(
            src_ref=src, dst_ref=qn.at[1 - s, j, piece, :],
            send_sem=n_ssem.at[s, d, j], recv_sem=n_rsem.at[1 - s, d, j],
            device_id=(side_id[s], h), device_id_type=pl.DeviceIdType.MESH)

    def query_in(s, d, j):
        dst = qn.at[s, j, row_block(from_head(d)), :]
        return pltpu.make_async_remote_copy(
            src_ref=dst, dst_ref=dst,
            send_sem=n_ssem.at[s, d, j], recv_sem=n_rsem.at[s, d, j],
            device_id=(side_id[s], h), device_id_type=pl.DeviceIdType.MESH)

    def part_out(s, j):
        return [
            pltpu.make_async_remote_copy(
                src_ref=src.at[s, j], dst_ref=dst.at[1 - s, j],
                send_sem=ss.at[s, j], recv_sem=rs.at[1 - s, j],
                device_id=(side_id[s], h), device_id_type=pl.DeviceIdType.MESH)
            for src, dst, ss, rs in ((po, pi, p_ssem, p_rsem), (lo, li, l_ssem, l_rsem))
        ]

    def part_in(s, j):
        return [
            pltpu.make_async_remote_copy(
                src_ref=dst.at[s, j], dst_ref=dst.at[s, j],
                send_sem=ss.at[s, j], recv_sem=rs.at[s, j],
                device_id=(side_id[s], h), device_id_type=pl.DeviceIdType.MESH)
            for dst, ss, rs in ((pi, p_ssem, p_rsem), (li, l_ssem, l_rsem))
        ]

    def result_out(d, j):
        to = at_head(d)
        return pltpu.make_async_remote_copy(
            src_ref=ob.at[j, row_block(to), :], dst_ref=out_ref.at[:, columns(h, j)],
            send_sem=o_ssem.at[d - 1, j], recv_sem=o_rsem.at[d - 1, j],
            device_id=(c, to), device_id_type=pl.DeviceIdType.MESH)

    def result_in(d, j):
        dst = out_ref.at[:, columns(from_head(d), j)]
        return pltpu.make_async_remote_copy(
            src_ref=dst, dst_ref=dst,
            send_sem=o_ssem.at[d - 1, j], recv_sem=o_rsem.at[d - 1, j],
            device_id=(c, from_head(d)), device_id_type=pl.DeviceIdType.MESH)

    def result_local(j):
        return pltpu.make_async_copy(
            ob.at[j, row_block(h), :], out_ref.at[:, columns(h, j)], oloc_sem.at[j])

    barrier = pltpu.get_barrier_semaphore()
    for d in range(1, n_head):
        pl.semaphore_signal(barrier, inc=1, device_id=(c, at_head(d)), device_id_type=pl.DeviceIdType.MESH)
    for s in range(2):
        @pl.when(has[s])
        def _():
            pl.semaphore_signal(barrier, inc=1, device_id=(side_id[s], h), device_id_type=pl.DeviceIdType.MESH)

    @pl.loop(0, nch)
    def _(j):
        for copy in local_in(j):
            copy.start()

    for s in range(3):
        source = jnp.clip(c + (-1, 1, 0)[s], 0, n_ctx - 1)
        for t in range(tiles_here):
            g = source * tiles_here + t
            used = reached_ref[g]
            for b in range(tiles_here):
                away = g - (c * tiles_here + b)
                near = jnp.where((away >= -2) & (away <= 2), 0.0, NEGATIVE)
                bias[s, pl.ds(b, 1), pl.ds(t * TILE, TILE)] = jnp.full((1, TILE), near, jnp.float32)
            for b in range(cache_tiles):
                times = jnp.int32(0)
                for r in range(REACH):
                    hit = (pattern_ref[g, r] == c * cache_tiles + b) & (r < used)
                    times = times + jnp.where(hit, 1, 0)
                log = jnp.float32(NEGATIVE)
                for n in range(1, REACH + 1):
                    log = jnp.where(times == n, jnp.float32(math.log2(n)), log)
                bias[s, pl.ds(tiles_here + b, 1), pl.ds(t * TILE, TILE)] = jnp.full((1, TILE), log, jnp.float32)

    peers = n_head - 1 + jnp.where(has[0], 1, 0) + jnp.where(has[1], 1, 0)
    pl.semaphore_wait(barrier, peers)

    for s in range(2):
        @pl.when(jnp.logical_not(has[s]))
        def _():
            @pl.loop(0, nch)
            def _(j):
                qn[s, j] = jnp.zeros(qn.shape[2:], qn.dtype)
                pi[s, j] = jnp.zeros(pi.shape[2:], pi.dtype)
                li[s, j] = jnp.full(li.shape[2:], NEGATIVE, li.dtype)

    def send_queries(j):
        for d in range(1, n_head):
            exchange(0, d, j).start()
        for s in range(2):
            @pl.when(has[s])
            def _():
                query_out(s, 0, j).start()

    def send_chunk(j):
        @pl.when(j + lead < nch)
        def _():
            send_queries(j + lead)

        for u in (1, 2):
            for d in range(1, n_head):
                exchange(u, d, j).start()

    ahead = min(AHEAD, nch)
    lead = min(LEAD, nch)

    @pl.loop(0, lead)
    def _(j):
        send_queries(j)

    @pl.loop(0, ahead)
    def _(j):
        send_chunk(j)

    scale = HD ** -0.5 * LOG2E

    def partial(s, near, far):
        blocks, gains, peak = [], [], None
        for b in range(tiles_here + cache_tiles):
            block = near[b * TILE:(b + 1) * TILE] if b < tiles_here else (
                far[(b - tiles_here) * TILE:(b - tiles_here + 1) * TILE])
            gain = bias[s, pl.ds(b, 1), :]
            tall = jnp.max(block, axis=0, keepdims=True) * scale + gain
            peak = tall if peak is None else jnp.maximum(peak, tall)
            blocks.append(block)
            gains.append(gain)
        total, weights = 0.0, []
        for block, gain in zip(blocks, gains):
            expos = jnp.exp2(block * scale + (gain - peak))
            total = total + jnp.sum(expos, axis=0, keepdims=True)
            weights.append(expos.astype(jnp.bfloat16))
        weights = jnp.concatenate(weights, axis=0)
        return weights, peak, total

    def relay(j):
        for d in range(1, n_head):
            exchange_in(0, d, j).wait_recv()
            for s in range(2):
                @pl.when(has[s])
                def _():
                    query_out(s, d, j).start()

    def attend(j):
        for copy in local_in(j):
            copy.wait()
        for t in (1, 2):
            for d in range(1, n_head):
                exchange_in(t, d, j).wait_recv()
        for s in range(2):
            @pl.when(has[s])
            def _():
                for d in range(n_head):
                    query_in(s, d, j).wait_recv()
        turned, raw, soft = {}, {}, {}

        def score(i, s):
            cols = slice(i * HD, (i + 1) * HD)
            if s == 0:
                turned[i] = jnp.concatenate([vs[j, :, cols].T, cvs[j, :, cols].T], axis=1)
            q = qs[j, :, cols] if s == 2 else qn[s, j, :, cols]
            raw[i, s] = (lax.dot_general(ks[j, :, cols], q, NT, preferred_element_type=jnp.float32),
                         lax.dot_general(cks[j, :, cols], q, NT, preferred_element_type=jnp.float32))

        def weigh(i, s):
            soft[i, s] = partial(s, *raw.pop((i, s)))

        def gather(i, s):
            weights, peak, total = soft.pop((i, s))
            summed = lax.dot_general(turned[i], weights, NN, preferred_element_type=jnp.float32)
            if s < 2:
                po[s, j, i] = (summed * (1.0 / total)).astype(jnp.bfloat16)
                lo[s, j, pl.ds(i, 1), :] = peak + jnp.log2(total)
            else:
                oacc[j, i] = summed
                macc[j, pl.ds(i, 1), :] = peak
                lacc[j, pl.ds(i, 1), :] = total

        def run(units):
            for n in range(len(units) + 2):
                if n < len(units):
                    score(*units[n])
                if n >= 2:
                    gather(*units[n - 2])
                if 1 <= n <= len(units):
                    weigh(*units[n - 1])

        run([(i, s) for i in range(hc) for s in range(2)])
        for s in range(2):
            @pl.when(has[s])
            def _():
                for copy in part_out(s, j):
                    copy.start()
        run([(i, 2) for i in range(hc)])

    def combine(j):
        for s in range(2):
            @pl.when(has[s])
            def _():
                for copy in part_in(s, j):
                    copy.wait_recv()
        for i in range(hc):
            m_own, m_low, m_high = macc[j, pl.ds(i, 1), :], li[0, j, pl.ds(i, 1), :], li[1, j, pl.ds(i, 1), :]
            top = jnp.maximum(m_own, jnp.maximum(m_low, m_high))
            f_own, f_low, f_high = jnp.exp2(m_own - top), jnp.exp2(m_low - top), jnp.exp2(m_high - top)
            inverse = 1.0 / (f_own * lacc[j, pl.ds(i, 1), :] + f_low + f_high)
            mixed = (oacc[j, i] * (f_own * inverse) + pi[0, j, i].astype(jnp.float32) * (f_low * inverse)
                     + pi[1, j, i].astype(jnp.float32) * (f_high * inverse))
            gain = gate_ref[pl.ds(h * (width // HD) + j * hc + i, 1), :]
            ob[j, :, i * HD:(i + 1) * HD] = (mixed.T * gain).astype(jnp.bfloat16)
        for d in range(1, n_head):
            result_out(d, j).start()
        result_local(j).start()

    @pl.loop(0, nch + 2)
    def _(i):
        @pl.when(i + ahead < nch)
        def _():
            send_chunk(i + ahead)

        @pl.when(i < nch)
        def _():
            relay(i)

        @pl.when((i >= 1) & (i <= nch))
        def _():
            attend(i - 1)

        @pl.when(i >= 2)
        def _():
            combine(i - 2)

    @pl.loop(0, nch)
    def _(j):
        for t in range(3):
            for d in range(1, n_head):
                exchange(t, d, j).wait_send()
        for s in range(2):
            @pl.when(has[s])
            def _():
                for d in range(n_head):
                    query_out(s, d, j).wait_send()
                for copy in part_out(s, j):
                    copy.wait_send()
        for d in range(1, n_head):
            result_out(d, j).wait_send()
            result_in(d, j).wait_recv()
        result_local(j).wait()


def local(n_ctx, n_head, queries, keys, values, cache_keys, cache_values, pattern, reached, gate):
    rows, model = queries.shape
    width = cache_keys.shape[1]
    heads_here = width // HD
    hc = max(n for n in range(1, GROUP + 1) if heads_here % n == 0)
    cw = hc * HD
    nch = heads_here // hc
    all_rows = rows * n_head
    tiles_here = all_rows // TILE
    cache_rows = cache_keys.shape[0]
    cache_tiles = cache_rows // TILE
    sizes = (n_ctx, n_head, rows, width, cw, hc, nch, tiles_here, cache_tiles)
    bf, f32 = jnp.bfloat16, jnp.float32
    dma = pltpu.SemaphoreType.DMA
    hbm = pl.BlockSpec(memory_space=pl.ANY)
    smem = pl.BlockSpec(memory_space=pltpu.SMEM)
    own = max(n_head - 1, 1)
    return pl.pallas_call(
        functools.partial(kernel, sizes),
        out_shape=jax.ShapeDtypeStruct((rows, model), bf),
        in_specs=[hbm] * 5 + [smem, smem, pl.BlockSpec(memory_space=pltpu.VMEM)],
        out_specs=hbm,
        scratch_shapes=[
            pltpu.VMEM((nch, all_rows, cw), bf),
            pltpu.VMEM((nch, all_rows, cw), bf),
            pltpu.VMEM((nch, all_rows, cw), bf),
            pltpu.VMEM((nch, cache_rows, cw), bf),
            pltpu.VMEM((nch, cache_rows, cw), bf),
            pltpu.VMEM((2, nch, all_rows, cw), bf),
            pltpu.VMEM((2, nch, hc, HD, all_rows), bf),
            pltpu.VMEM((2, nch, hc, HD, all_rows), bf),
            pltpu.VMEM((2, nch, 8, all_rows), f32),
            pltpu.VMEM((2, nch, 8, all_rows), f32),
            pltpu.VMEM((nch, hc, HD, all_rows), f32),
            pltpu.VMEM((nch, 8, all_rows), f32),
            pltpu.VMEM((nch, 8, all_rows), f32),
            pltpu.VMEM((nch, all_rows, cw), bf),
            pltpu.VMEM((3, -(-(tiles_here + cache_tiles) // 8) * 8, all_rows), f32),
            dma((5, nch)),
            dma((3, own, nch)), dma((3, own, nch)),
            dma((2, n_head, nch)), dma((2, n_head, nch)),
            dma((2, nch)), dma((2, nch)),
            dma((2, nch)), dma((2, nch)),
            dma((own, nch)), dma((own, nch)),
            dma((nch,)),
        ],
        compiler_params=pltpu.CompilerParams(
            collective_id=0, has_side_effects=True, vmem_limit_bytes=56 * 1024 * 1024),
    )(queries, keys, values, cache_keys, cache_values, pattern, reached, gate.reshape(model // HD, HD))


def solution(mesh):
    placed = (
        P(("ctx", "head"), None),
        P(("ctx", "head"), None),
        P(("ctx", "head"), None),
        P("ctx", "head"),
        P("ctx", "head"),
        P(),
        P(),
        P(),
    )
    return jax.shard_map(
        functools.partial(local, mesh.shape["ctx"], mesh.shape["head"]),
        mesh=mesh, in_specs=placed, out_specs=P(("ctx", "head"), None), check_vma=False
    )
```
